128 devices in a mesh: row: 4 (over z), col: 32 (over y, x, core).
Axes of the slice: x: 4, y: 4, z: 4, core: 2. Of those that a mesh axis runs over, the one named last changes fastest.
Arguments:
- tokens: bfloat16 [1024, 12288], P('col', 'row'), may hold values from -6 to 6
- cotangent: bfloat16 [1024, 12288], P('col', 'row'), may hold values from -4 to 4
- weight_in: bfloat16 [12288, 24576], P('row', 'col'), may hold values from -0.0546875 to 0.0546875
- bias_in: float32 [24576], P('col'), may hold values from -4 to 4
- weight_out: bfloat16 [24576, 12288], P('col', 'row'), may hold values from -0.0390625 to 0.0390625
Outputs:
- grad_tokens: bfloat16 [1024, 12288], P('col', 'row')
- grad_weight_in: bfloat16 [12288, 24576], P('row', 'col')
- grad_bias_in: float32 [24576], P('col')
- grad_weight_out: bfloat16 [24576, 12288], P('col', 'row')
- grad_bias_out: float32 [12288], P('row')
The draws below stay inside these ranges and needn't reach their ends.
All inputs are finite; a program needn't handle non-finite values.
Results may differ from the reference program's by a relative error of at most 0.007.
Values may be sent and summed in bfloat16 or wider, within the bound.
A program may use at most 128 MiB of HBM per device.

```python
import jax
import jax.numpy as jnp
from jax import lax

D = 12288
FF = 24576
TOKENS = 1024


def levels(rng, extent, pieces, least, high):
    level = 1.0
    for axis_at, blocks in pieces:
        heights = jax.random.uniform(jax.random.fold_in(jax.random.fold_in(rng, 6), axis_at), (blocks,), jnp.float32, least / len(pieces), high / len(pieces))
        level = level * jnp.repeat(jnp.exp(heights), extent[axis_at] // blocks).reshape((-1,) + (1,) * (len(extent) - 1 - axis_at))
    return level


def scatter_about(rng, dims, spread, limit, shards=(), held_as=jnp.bfloat16):
    factor_of = levels(rng, dims, shards, -0.22, 0.18) if shards else 1.0
    values = jax.random.normal(rng, dims, jnp.float32) * spread * factor_of
    return jnp.minimum(jnp.maximum(values, -limit), limit).astype(held_as)


def setup_inputs(seed: int = 0) -> dict:
    seeds = jax.random.split(jax.random.key(seed), 6)
    return {
        "tokens": scatter_about(seeds[0], (TOKENS, D), 1.0, 6.0, ((0, 32), (1, 4))),
        "cotangent": scatter_about(seeds[1], (TOKENS, D), 0.5, 4.0, ((0, 32), (1, 4))),
        "weight_in": scatter_about(seeds[2], (D, FF), D ** -0.5, 0.0546875, ((0, 4), (1, 32))),
        "bias_in": scatter_about(seeds[3], (FF,), 1.0, 4.0, ((0, 32),), jnp.float32),
        "weight_out": scatter_about(seeds[4], (FF, D), FF ** -0.5, 0.0390625, ((0, 32), (1, 4))),
    }


coeff = 0.7978845608


def act_parts(preact, hidden_grad):
    cube = preact * preact * preact
    tangent = jnp.tanh(coeff * (preact + 0.044715 * cube))
    activated = (0.5 * preact * (1.0 + tangent)).astype(jnp.bfloat16)
    slope = 0.5 * (1.0 + tangent) + 0.5 * preact * (1.0 - tangent * tangent) * coeff * (1.0 + 0.134145 * preact * preact)
    return activated, (hidden_grad * slope).astype(jnp.bfloat16)


def reference(tokens, cotangent, weight_in, bias_in, weight_out):
    preact = jnp.dot(tokens, weight_in, preferred_element_type=jnp.float32) + bias_in
    hidden_grad = lax.dot_general(cotangent, weight_out, (((1,), (1,)), ((), ())), preferred_element_type=jnp.float32)
    activated, preact_grad = act_parts(preact, hidden_grad)
    grad_weight_out = lax.dot_general(activated, cotangent, (((0,), (0,)), ((), ())), preferred_element_type=jnp.float32).astype(jnp.bfloat16)
    grad_bias_out = jnp.sum(cotangent.astype(jnp.float32), axis=0)
    grad_weight_in = lax.dot_general(tokens, preact_grad, (((0,), (0,)), ((), ())), preferred_element_type=jnp.float32).astype(jnp.bfloat16)
    grad_bias_in = jnp.sum(preact_grad.astype(jnp.float32), axis=0)
    grad_tokens = lax.dot_general(preact_grad, weight_in, (((1,), (1,)), ((), ())), preferred_element_type=jnp.float32).astype(jnp.bfloat16)
    return grad_tokens, grad_weight_in, grad_bias_in, grad_weight_out, grad_bias_out
```

```python
import jax
import jax.numpy as jnp
from jax import lax
from jax.experimental import pallas as pl
from jax.experimental.pallas import tpu as pltpu
from jax.sharding import PartitionSpec as P

MESH = pl.DeviceIdType.MESH
coeff = 0.7978845608
N_COPIES = 112
D1 = (0, 1, 3, 2)
CHUNKS = (
    tuple((d, 0) for d in D1),
    ((0, 1), (1, 1), (0, 3), (1, 3)),
    ((3, 1), (2, 1), (3, 3), (2, 3)),
    tuple((d, 2) for d in D1),
)
ROW = {b: c * 256 + i * 32 for c, blocks in enumerate(CHUNKS) for i, b in enumerate(blocks)}


def act_parts(preact, hidden_grad):
    cube = preact * preact * preact
    tangent = jnp.tanh(coeff * (preact + 0.044715 * cube))
    activated = (0.5 * preact * (1.0 + tangent)).astype(jnp.bfloat16)
    slope = 0.5 * (1.0 + tangent) + 0.5 * preact * (1.0 - tangent * tangent) * coeff * (
        1.0 + 0.134145 * preact * preact
    )
    return (activated, (hidden_grad * slope).astype(jnp.bfloat16))


def dot(a, b, ca, cb):
    return lax.dot_general(a, b, (((ca,), (cb,)), ((), ())), preferred_element_type=jnp.float32)


def kernel(
    tok_hbm, cot_hbm, win_hbm, bias_ref, wout_hbm,
    gtok_ref, gwin_hbm, gbin_ref, gwout_hbm, gbout_ref,
    tc, wi, wo, pb, zr, ag, gt, ex, rr, q2, r2, fin, lsem, ssem, rsem,
):
    z = lax.axis_index("row")
    col = lax.axis_index("col")
    y, x, k = col // 8, (col // 2) % 4, col % 2

    def dev(d1=0, d2=0, dz=0, dk=0):
        dx, dy = d1 * (1 - k) + d2 * k, d1 * k + d2 * (1 - k)
        return ((z + dz) % 4, ((y + dy) % 4) * 8 + ((x + dx) % 4) * 2 + (k + dk) % 2)

    used = [0]
    sent = []

    def describe(i, src, dst, device):
        return pltpu.make_async_remote_copy(
            src_ref=src, dst_ref=dst, send_sem=ssem.at[i], recv_sem=rsem.at[i], device_id=device, device_id_type=MESH
        )

    def send(src, dst, device):
        i = used[0]
        used[0] += 1
        cp = describe(i, src, dst, device)
        cp.start()
        sent.append(cp)
        return cp, i

    loads = [
        pltpu.make_async_copy(tok_hbm, tc.at[0, pl.ds(0, 32)], lsem.at[0]),
        pltpu.make_async_copy(cot_hbm, tc.at[1, pl.ds(0, 32)], lsem.at[1]),
        pltpu.make_async_copy(win_hbm, wi, lsem.at[2]),
        pltpu.make_async_copy(wout_hbm, wo, lsem.at[3]),
    ]
    for cp in loads:
        cp.start()

    barrier = pltpu.get_barrier_semaphore()
    greeted = [dev(dk=1)]
    for o in (1, 2, 3):
        greeted += [dev(d1=o), dev(d2=o), dev(dz=o)]
    for device in greeted:
        pl.semaphore_signal(barrier, inc=1, device_id=device, device_id_type=MESH)
    pl.semaphore_wait(barrier, len(greeted))
    loads[0].wait()
    loads[1].wait()

    def block(row):
        return tc.at[:, pl.ds(row, 32)]

    p1, p2, sib = {}, {}, {}

    def share(b):
        sib[b] = send(block(ROW[b]), block(ROW[b] + 128), dev(dk=1))[0]

    for o in (1, 3, 2):
        p1[(-o) % 4] = send(block(0), block(ROW[(-o) % 4, 0]), dev(d1=o))[0]
    share((0, 0))

    def spread(d1):
        for o in (1, 3):
            d2 = (-o) % 4
            p2[d1, d2] = send(block(ROW[d1, 0]), block(ROW[d1, d2]), dev(d2=o))[0]

    def arrive(d1, d2):
        p2[d1, d2].wait_recv()
        if (d2 == 1 and d1 in (0, 3)) or (d2 == 3 and d1 in (1, 2)):
            o = (d2 + 2) % 4
            p2[d1, 2] = send(block(ROW[d1, d2]), block(ROW[d1, 2]), dev(d2=o))[0]
        share((d1, d2))

    zs, agd, fwd2 = {}, {}, {}

    def forward(c):
        for b in CHUNKS[c]:
            sib[b].wait_recv()
        rows = pl.ds(c * 256, 256)
        pb[c, :, 0] = dot(tc[0, rows, :], wi[...], 1, 0).astype(jnp.bfloat16).reshape(4, 64, 768)
        pb[c, :, 1] = dot(tc[1, rows, :], wo[...], 1, 1).astype(jnp.bfloat16).reshape(4, 64, 768)
        for o in (1, 3, 2):
            s = (-o) % 4
            zs[c, s] = send(pb.at[c, (z + o) % 4], zr.at[c, s - 1], dev(dz=o))[0]
        part = jnp.sum(tc[1, rows, :].astype(jnp.float32), axis=0, keepdims=True)
        gbout_ref[...] = part if c == 0 else gbout_ref[...] + part

    def agrows(c, zz, start=0, n=64):
        return ag.at[:, pl.ds(pl.multiple_of(c * 256 + zz * 64 + start, 32), n)]

    def activate(c):
        for s in (1, 3, 2):
            zs[c, s].wait_recv()
        u = bias_ref[...] + pb[c, z, 0].astype(jnp.float32)
        h = pb[c, z, 1].astype(jnp.float32)
        for s in range(3):
            u += zr[c, s, 0].astype(jnp.float32)
            h += zr[c, s, 1].astype(jnp.float32)
        activated, preact_grad = act_parts(u, h)
        mine = pl.ds(pl.multiple_of(c * 256 + z * 64, 64), 64)
        ag[0, mine, :] = activated
        ag[1, mine, :] = preact_grad
        for o in (1, 3):
            agd[c, (-o) % 4] = send(agrows(c, z), agrows(c, z), dev(dz=o))[1]

    def relay(c):
        for s, start in ((1, 0), (3, 32)):
            zz = (z + s) % 4
            describe(agd[c, s], agrows(c, zz), agrows(c, zz), dev(dz=s)).wait_recv()
            fwd2[c, s] = send(agrows(c, zz, start, 32), agrows(c, zz, start, 32), dev(dz=(s + 2) % 4))[1]

    def gathered(c):
        zz = (z + 2) % 4
        for s, start in ((1, 0), (3, 32)):
            half = agrows(c, zz, start, 32)
            describe(fwd2[c, s], half, half, dev(dz=2)).wait_recv()

    exd, rrd = {}, []

    def token_grad(c):
        gathered(c)
        pg = ag[1, pl.ds(c * 256, 256), :]

        @pl.loop(0, 4)
        def _(n):
            cols = pl.ds(pl.multiple_of(n * 768, 768), 768)
            gt[pl.ds(c * 256, 256), cols] = dot(pg, wi[cols, :], 1, 1).astype(jnp.bfloat16)

        exd[c] = send(gt.at[pl.ds(c * 256 + 128, 128)], ex.at[c], dev(dk=1))[0]
        part = jnp.sum(pg.astype(jnp.float32), axis=0, keepdims=True)
        gbin_ref[...] = part if c == 0 else gbin_ref[...] + part

    def combine(c):
        exd[c].wait_recv()
        own = pl.ds(c * 256, 128)
        gt[own, :] = (gt[own, :].astype(jnp.float32) + ex[c].astype(jnp.float32)).astype(jnp.bfloat16)
        if c == 3:
            rrd.append(send(gt.at[own], rr.at[1], dev(d2=2))[0])
        elif c > 0:
            for i, d2 in enumerate((1, 3)):
                src = gt.at[pl.ds(c * 256 + i * 64, 64)]
                rrd.append(send(src, rr.at[(-d2) % 4 - 1, pl.ds((c - 1) * 64, 64)], dev(d2=d2))[0])

    spread(0)
    p1[1].wait_recv()
    share((1, 0))
    spread(1)
    p1[3].wait_recv()
    share((3, 0))
    p1[2].wait_recv()
    share((2, 0))
    spread(3)
    spread(2)
    loads[2].wait()
    loads[3].wait()
    forward(0)
    for b in CHUNKS[1]:
        arrive(*b)
    forward(1)
    activate(0)
    for b in CHUNKS[2]:
        arrive(*b)
    forward(2)
    activate(1)
    relay(0)
    for d1 in D1:
        p2[d1, 2].wait_recv()
        share((d1, 2))
    forward(3)
    activate(2)
    relay(1)
    token_grad(0)
    activate(3)
    relay(2)
    token_grad(1)
    combine(0)
    combine(1)
    relay(3)
    token_grad(2)
    combine(2)
    token_grad(3)
    combine(3)

    @pl.loop(0, 12)
    def _(n):
        cols = pl.ds(pl.multiple_of(n * 256, 256), 256)
        wo[:, cols] = dot(ag[0], tc[1, :, cols], 0, 0).astype(jnp.bfloat16)

    out_wo = pltpu.make_async_copy(wo, gwout_hbm, lsem.at[0])
    out_wo.start()

    for cp in rrd:
        cp.wait_recv()
    r2d = []
    for i, d1 in enumerate(D1):
        rows = pl.ds(i * 32, 32)
        total = gt[rows, :].astype(jnp.float32)
        for s in range(3):
            total += rr[s, rows, :].astype(jnp.float32)
        if d1 == 0:
            fin[...] = total
        else:
            q2[d1 - 1] = total.astype(jnp.bfloat16)
            r2d.append(send(q2.at[d1 - 1], r2.at[(-d1) % 4 - 1], dev(d1=d1))[0])

    @pl.loop(0, 4)
    def _(m):
        cols = pl.ds(pl.multiple_of(m * 768, 768), 768)
        wi[cols, :] = dot(tc[0, :, cols], ag[1], 0, 0).astype(jnp.bfloat16)

    out_wi = pltpu.make_async_copy(wi, gwin_hbm, lsem.at[1])
    out_wi.start()
    for cp in r2d:
        cp.wait_recv()
    total = fin[...]
    for s in range(3):
        total += r2[s].astype(jnp.float32)
    gtok_ref[...] = total.astype(jnp.bfloat16)
    for cp in sent:
        cp.wait_send()
    out_wo.wait()
    out_wi.wait()


def per_device(tokens, cotangent, weight_in, bias_in, weight_out):
    vmem, hbm = pl.BlockSpec(memory_space=pltpu.VMEM), pl.BlockSpec(memory_space=pl.ANY)
    bf16, f32 = jnp.bfloat16, jnp.float32
    grad_tokens, grad_weight_in, grad_bias_in, grad_weight_out, grad_bias_out = pl.pallas_call(
        kernel,
        out_shape=(
            jax.ShapeDtypeStruct((32, 3072), bf16),
            jax.ShapeDtypeStruct((3072, 768), bf16),
            jax.ShapeDtypeStruct((1, 768), f32),
            jax.ShapeDtypeStruct((768, 3072), bf16),
            jax.ShapeDtypeStruct((1, 3072), f32),
        ),
        in_specs=[hbm, hbm, hbm, vmem, hbm],
        out_specs=(vmem, hbm, vmem, hbm, vmem),
        scratch_shapes=[
            pltpu.VMEM((2, 1024, 3072), bf16),
            pltpu.VMEM((3072, 768), bf16),
            pltpu.VMEM((768, 3072), bf16),
            pltpu.VMEM((4, 4, 2, 64, 768), bf16),
            pltpu.VMEM((4, 3, 2, 64, 768), bf16),
            pltpu.VMEM((2, 1024, 768), bf16),
            pltpu.VMEM((1024, 3072), bf16),
            pltpu.VMEM((4, 128, 3072), bf16),
            pltpu.VMEM((3, 128, 3072), bf16),
            pltpu.VMEM((3, 32, 3072), bf16),
            pltpu.VMEM((3, 32, 3072), bf16),
            pltpu.VMEM((32, 3072), f32),
            pltpu.SemaphoreType.DMA((4,)),
            pltpu.SemaphoreType.DMA((N_COPIES,)),
            pltpu.SemaphoreType.DMA((N_COPIES,)),
        ],
        compiler_params=pltpu.CompilerParams(
            collective_id=0, has_side_effects=True, vmem_limit_bytes=60 * 2**20
        ),
        cost_estimate=pl.CostEstimate(flops=24_200_000_000, bytes_accessed=20_000_000, transcendentals=800_000),
    )(tokens, cotangent, weight_in, bias_in.reshape(1, 768), weight_out)
    return (
        grad_tokens,
        grad_weight_in,
        grad_bias_in.reshape(768),
        grad_weight_out,
        grad_bias_out.reshape(3072),
    )


def solution(mesh):
    placed = (P("col", "row"), P("col", "row"), P("row", "col"), P("col"), P("col", "row"))
    return jax.shard_map(
        per_device,
        mesh=mesh,
        in_specs=placed,
        out_specs=(P("col", "row"), P("row", "col"), P("col"), P("col", "row"), P("row")),
        check_vma=False,
    )
```

```python
import jax
import jax.numpy as jnp
from jax import lax
from jax.experimental import pallas as pl
from jax.experimental.pallas import tpu as pltpu
from jax.sharding import PartitionSpec as P

MESH = pl.DeviceIdType.MESH
coeff = 0.7978845608
N_COPIES = 112
D1 = (0, 1, 3, 2)
CHUNKS = (
    tuple((d, 0) for d in D1),
    ((0, 1), (1, 1), (0, 3), (1, 3)),
    ((3, 1), (2, 1), (3, 3), (2, 3)),
    tuple((d, 2) for d in D1),
)
ROW = {b: c * 256 + i * 32 for c, blocks in enumerate(CHUNKS) for i, b in enumerate(blocks)}


def act_parts(preact, hidden_grad):
    cube = preact * preact * preact
    tangent = jnp.tanh(coeff * (preact + 0.044715 * cube))
    activated = (0.5 * preact * (1.0 + tangent)).astype(jnp.bfloat16)
    slope = 0.5 * (1.0 + tangent) + 0.5 * preact * (1.0 - tangent * tangent) * coeff * (
        1.0 + 0.134145 * preact * preact
    )
    return (activated, (hidden_grad * slope).astype(jnp.bfloat16))


def dot(a, b, ca, cb):
    return lax.dot_general(a, b, (((ca,), (cb,)), ((), ())), preferred_element_type=jnp.float32)


def kernel(
    tok_hbm, cot_hbm, win_hbm, bias_hbm, wout_hbm,
    gtok_ref, wi, gbin_ref, wo, gbout_ref,
    bias, tc, pb, za, zr, ag, gt, ex, rr, q2, r2, fin, lsem, ssem, rsem,
):
    z = lax.axis_index("row")
    col = lax.axis_index("col")
    y, x, k = col // 8, (col // 2) % 4, col % 2

    def dev(d1=0, d2=0, dz=0, dk=0):
        dx, dy = d1 * (1 - k) + d2 * k, d1 * k + d2 * (1 - k)
        return ((z + dz) % 4, ((y + dy) % 4) * 8 + ((x + dx) % 4) * 2 + (k + dk) % 2)

    used = [0]
    sent = []

    def describe(i, src, dst, device):
        return pltpu.make_async_remote_copy(
            src_ref=src, dst_ref=dst, send_sem=ssem.at[i], recv_sem=rsem.at[i], device_id=device, device_id_type=MESH
        )

    def send(src, dst, device):
        i = used[0]
        used[0] += 1
        cp = describe(i, src, dst, device)
        cp.start()
        sent.append(cp)
        return cp, i

    loads = [
        pltpu.make_async_copy(tok_hbm, tc.at[0, pl.ds(0, 32)], lsem.at[0]),
        pltpu.make_async_copy(cot_hbm, tc.at[1, pl.ds(0, 32)], lsem.at[1]),
        pltpu.make_async_copy(win_hbm, wi, lsem.at[2]),
        pltpu.make_async_copy(wout_hbm, wo, lsem.at[3]),
        pltpu.make_async_copy(bias_hbm, bias.at[0], lsem.at[4]),
    ]
    for cp in loads:
        cp.start()

    barrier = pltpu.get_barrier_semaphore()
    greeted = [dev(dk=1)]
    for o in (1, 2, 3):
        greeted += [dev(d1=o), dev(d2=o), dev(dz=o)]
    for device in greeted:
        pl.semaphore_signal(barrier, inc=1, device_id=device, device_id_type=MESH)
    pl.semaphore_wait(barrier, len(greeted))

    def block(row):
        return tc.at[:, pl.ds(row, 32)]

    p1, p2, sib = {}, {}, {}

    def share(b):
        sib[b] = send(block(ROW[b]), block(ROW[b] + 128), dev(dk=1))[0]

    for o in (1, 3, 2):
        rows = pl.ds(ROW[(-o) % 4, 0], 32)
        p1[(-o) % 4] = [send(own, tc.at[i, rows], dev(d1=o))[0] for i, own in enumerate((tok_hbm, cot_hbm))]
    loads[0].wait()
    loads[1].wait()
    share((0, 0))

    def first(d1):
        for cp in p1[d1]:
            cp.wait_recv()
        share((d1, 0))

    def spread(d1):
        for o in (1, 3):
            d2 = (-o) % 4
            p2[d1, d2] = send(block(ROW[d1, 0]), block(ROW[d1, d2]), dev(d2=o))[0]

    def arrive(d1, d2):
        p2[d1, d2].wait_recv()
        if (d2 == 1 and d1 in (0, 3)) or (d2 == 3 and d1 in (1, 2)):
            o = (d2 + 2) % 4
            p2[d1, 2] = send(block(ROW[d1, d2]), block(ROW[d1, 2]), dev(d2=o))[0]
        share((d1, d2))

    zs, agd, fwd2 = {}, {}, {}
    low, high = pl.ds(0, 32), pl.ds(32, 32)

    def part(c, zz, half):
        return pb.at[c, zz % 4, :, half]

    def forward(c):
        for b in CHUNKS[c]:
            sib[b].wait_recv()
        rows = pl.ds(c * 256, 256)
        pb[c, :, 0] = dot(tc[0, rows, :], wi[...], 1, 0).astype(jnp.bfloat16).reshape(4, 64, 768)
        pb[c, :, 1] = dot(tc[1, rows, :], wo[...], 1, 1).astype(jnp.bfloat16).reshape(4, 64, 768)
        for i, (o, near, far) in enumerate(((1, high, low), (3, low, high))):
            zs[c, i, "far"] = send(part(c, z + 2, far), za.at[c, i], dev(dz=o))[0]
            zs[c, i, "near"] = send(part(c, z + o, near), zr.at[c, i, :, near], dev(dz=o))[0]
        total = jnp.sum(tc[1, rows, :].astype(jnp.float32), axis=0, keepdims=True)
        gbout_ref[...] = total if c == 0 else gbout_ref[...] + total

    def pass_on(c):
        for i, (o, far) in enumerate(((1, low), (3, high))):
            zs[c, i, "far"].wait_recv()
            there = (z + o) % 4
            both = pb[c, there, :, far].astype(jnp.float32) + za[c, i].astype(jnp.float32)
            pb[c, there, :, far] = both.astype(jnp.bfloat16)
            zs[c, i, "sum"] = send(part(c, z + o, far), zr.at[c, i, :, far], dev(dz=o))[0]

    def agrows(c, zz, start=0, n=64):
        return ag.at[:, pl.ds(pl.multiple_of(c * 256 + zz * 64 + start, 32), n)]

    def activate(c):
        for i in range(2):
            zs[c, i, "near"].wait_recv()
            zs[c, i, "sum"].wait_recv()
        u = bias[...] + pb[c, z, 0].astype(jnp.float32)
        h = pb[c, z, 1].astype(jnp.float32)
        for i in range(2):
            u += zr[c, i, 0].astype(jnp.float32)
            h += zr[c, i, 1].astype(jnp.float32)
        activated, preact_grad = act_parts(u, h)
        mine = pl.ds(pl.multiple_of(c * 256 + z * 64, 64), 64)
        ag[0, mine, :] = activated
        ag[1, mine, :] = preact_grad
        for o in (1, 3):
            agd[c, (-o) % 4] = send(agrows(c, z), agrows(c, z), dev(dz=o))[1]

    def relay(c):
        for s, start in ((1, 0), (3, 32)):
            zz = (z + s) % 4
            describe(agd[c, s], agrows(c, zz), agrows(c, zz), dev(dz=s)).wait_recv()
            fwd2[c, s] = send(agrows(c, zz, start, 32), agrows(c, zz, start, 32), dev(dz=(s + 2) % 4))[1]

    def gathered(c):
        zz = (z + 2) % 4
        for s, start in ((1, 0), (3, 32)):
            half = agrows(c, zz, start, 32)
            describe(fwd2[c, s], half, half, dev(dz=2)).wait_recv()

    exd, rrd = {}, []

    def token_grad(c):
        gathered(c)
        pg = ag[1, pl.ds(c * 256, 256), :]

        @pl.loop(0, 2)
        def _(n):
            cols = pl.ds(pl.multiple_of(n * 1536, 1536), 1536)
            gt[pl.ds(c * 256, 256), cols] = dot(pg, wi[cols, :], 1, 1).astype(jnp.bfloat16)

        exd[c] = send(gt.at[pl.ds(c * 256 + 128, 128)], ex.at[c], dev(dk=1))[0]
        part = jnp.sum(pg.astype(jnp.float32), axis=0, keepdims=True)
        gbin_ref[...] = part if c == 1 else gbin_ref[...] + part

    def combine(c):
        exd[c].wait_recv()
        own = pl.ds(c * 256, 128)
        gt[own, :] = (gt[own, :].astype(jnp.float32) + ex[c].astype(jnp.float32)).astype(jnp.bfloat16)
        if c == 3:
            rrd.append(send(gt.at[own], rr.at[1], dev(d2=2))[0])
        elif c > 0:
            for i, d2 in enumerate((1, 3)):
                src = gt.at[pl.ds(c * 256 + i * 64, 64)]
                rrd.append(send(src, rr.at[(-d2) % 4 - 1, pl.ds((c - 1) * 64, 64)], dev(d2=d2))[0])

    def end_scatter():
        for cp in rrd:
            cp.wait_recv()
        for i, d1 in enumerate(D1):
            rows = pl.ds(i * 32, 32)
            total = gt[rows, :].astype(jnp.float32)
            for s in range(3):
                total += rr[s, rows, :].astype(jnp.float32)
            if d1 == 0:
                fin[...] = total
            else:
                q2[d1 - 1] = total.astype(jnp.bfloat16)
                r2d.append(send(q2.at[d1 - 1], r2.at[(-d1) % 4 - 1], dev(d1=d1))[0])

    def weight_out_grad(n):
        cols = pl.ds(n * 768, 768)
        wo[:, cols] = dot(ag[0], tc[1, :, cols], 0, 0).astype(jnp.bfloat16)

    def weight_in_grad(n):
        cols = pl.ds(n * 768, 768)
        wi[cols, :] = dot(tc[0, :, cols], ag[1], 0, 0).astype(jnp.bfloat16)

    r2d = []
    first(1)
    first(3)
    spread(0)
    spread(1)
    first(2)
    spread(3)
    spread(2)
    loads[2].wait()
    loads[3].wait()
    loads[4].wait()
    forward(0)
    arrive(0, 1)
    arrive(0, 3)
    pass_on(0)
    arrive(1, 1)
    arrive(1, 3)
    forward(1)
    activate(0)
    arrive(3, 1)
    arrive(3, 3)
    pass_on(1)
    arrive(2, 1)
    arrive(2, 3)
    forward(2)
    activate(1)
    for d1 in D1:
        p2[d1, 2].wait_recv()
        share((d1, 2))
    pass_on(2)
    forward(3)
    relay(1)
    pass_on(3)
    token_grad(1)
    activate(3)
    combine(1)
    activate(2)
    relay(3)
    relay(2)
    token_grad(3)
    relay(0)
    combine(3)
    token_grad(2)
    token_grad(0)
    combine(2)
    combine(0)
    weight_out_grad(0)
    weight_out_grad(1)
    weight_out_grad(2)
    end_scatter()
    weight_out_grad(3)
    for n in range(4):
        weight_in_grad(n)
    for cp in r2d:
        cp.wait_recv()
    total = fin[...]
    for s in range(3):
        total += r2[s].astype(jnp.float32)
    gtok_ref[...] = total.astype(jnp.bfloat16)
    for cp in sent:
        cp.wait_send()


def store(*refs):
    sem = refs[10]
    moves = [pltpu.make_async_copy(refs[i], refs[5 + i], sem.at[i]) for i in (1, 3, 0)]
    moves += [pltpu.make_async_copy(refs[i].at[0], refs[5 + i], sem.at[i]) for i in (2, 4)]
    for cp in moves:
        cp.start()
    for cp in moves:
        cp.wait()


def per_device(tokens, cotangent, weight_in, bias_in, weight_out):
    hbm = pl.BlockSpec(memory_space=pl.ANY)
    bf16, f32 = jnp.bfloat16, jnp.float32
    kept = (((32, 3072), bf16), ((3072, 768), bf16), ((1, 768), f32), ((768, 3072), bf16), ((1, 3072), f32))
    results = pl.pallas_call(
        kernel,
        out_shape=tuple(pltpu.VMEM(shape, dtype) for shape, dtype in kept),
        in_specs=[hbm] * 5,
        out_specs=tuple(pl.BlockSpec(memory_space=pltpu.VMEM) for _ in kept),
        scratch_shapes=[
            pltpu.VMEM((1, 768), f32),
            pltpu.VMEM((2, 1024, 3072), bf16),
            pltpu.VMEM((4, 4, 2, 64, 768), bf16),
            pltpu.VMEM((4, 2, 2, 32, 768), bf16),
            pltpu.VMEM((4, 2, 2, 64, 768), bf16),
            pltpu.VMEM((2, 1024, 768), bf16),
            pltpu.VMEM((1024, 3072), bf16),
            pltpu.VMEM((4, 128, 3072), bf16),
            pltpu.VMEM((3, 128, 3072), bf16),
            pltpu.VMEM((3, 32, 3072), bf16),
            pltpu.VMEM((3, 32, 3072), bf16),
            pltpu.VMEM((32, 3072), f32),
            pltpu.SemaphoreType.DMA((5,)),
            pltpu.SemaphoreType.DMA((N_COPIES,)),
            pltpu.SemaphoreType.DMA((N_COPIES,)),
        ],
        compiler_params=pltpu.CompilerParams(
            collective_id=0, has_side_effects=True, vmem_limit_bytes=46 * 2**20
        ),
        cost_estimate=pl.CostEstimate(flops=24_200_000_000, bytes_accessed=20_000_000, transcendentals=800_000),
    )(tokens, cotangent, weight_in, bias_in, weight_out)
    return pl.pallas_call(
        store,
        out_shape=tuple(
            jax.ShapeDtypeStruct(shape[1:] if shape[0] == 1 else shape, dtype) for shape, dtype in kept
        ),
        in_specs=[pl.BlockSpec(memory_space=pltpu.VMEM)] * 5,
        out_specs=(hbm,) * 5,
        scratch_shapes=[pltpu.SemaphoreType.DMA((5,))],
        compiler_params=pltpu.CompilerParams(vmem_limit_bytes=2**20),
    )(*results)


def solution(mesh):
    placed = (P("col", "row"), P("col", "row"), P("row", "col"), P("col"), P("col", "row"))
    return jax.shard_map(
        per_device,
        mesh=mesh,
        in_specs=placed,
        out_specs=(P("col", "row"), P("row", "col"), P("col"), P("col", "row"), P("row")),
        check_vma=False,
    )
```

```python
import jax
import jax.numpy as jnp
from jax import lax
from jax.experimental import pallas as pl
from jax.experimental.pallas import tpu as pltpu
from jax.sharding import PartitionSpec as P

MESH = pl.DeviceIdType.MESH
coeff = 0.7978845608
N_COPIES = 160
D1 = (0, 1, 3, 2)
CHUNKS = (
    ((0, 0), (1, 0), (3, 0)),
    ((2, 0), (0, 1), (0, 3)),
    ((1, 1), (1, 3), (3, 1), (3, 3)),
    ((0, 2), (1, 2), (2, 1), (2, 3)),
    ((3, 2), (2, 2)),
)
SIZE = [64 * len(blocks) for blocks in CHUNKS]
ORDER = (0, 1, 4, 2, 3)
BASE = {c: sum(SIZE[d] for d in ORDER[:i]) for i, c in enumerate(ORDER)}
ROW = {b: BASE[c] + i * 32 for c, blocks in enumerate(CHUNKS) for i, b in enumerate(blocks)}
HALF = {b: SIZE[c] // 2 for c, blocks in enumerate(CHUNKS) for b in blocks}


def act_parts(preact, hidden_grad):
    cube = preact * preact * preact
    tangent = jnp.tanh(coeff * (preact + 0.044715 * cube))
    activated = (0.5 * preact * (1.0 + tangent)).astype(jnp.bfloat16)
    slope = 0.5 * (1.0 + tangent) + 0.5 * preact * (1.0 - tangent * tangent) * coeff * (
        1.0 + 0.134145 * preact * preact
    )
    return (activated, (hidden_grad * slope).astype(jnp.bfloat16))


def dot(a, b, ca, cb):
    return lax.dot_general(a, b, (((ca,), (cb,)), ((), ())), preferred_element_type=jnp.float32)


def kernel(
    tok_hbm, cot_hbm, win_hbm, bias_hbm, wout_hbm,
    gtok_ref, wi, gbin_ref, wo, gbout_ref,
    bias, tc, pb, za, zr, ag, gt, ex, rr, q2, r2, fin, acc, lsem, ssem, rsem,
):
    z = lax.axis_index("row")
    col = lax.axis_index("col")
    y, x, k = col // 8, (col // 2) % 4, col % 2

    def dev(d1=0, d2=0, dz=0, dk=0, turn=0):
        dx, dy = (d2, d1) if turn else (d1, d2)
        return ((z + dz) % 4, ((y + dy) % 4) * 8 + ((x + dx) % 4) * 2 + (k + dk) % 2)

    used = [0]
    sent = []

    def describe(i, src, dst, device):
        return pltpu.make_async_remote_copy(
            src_ref=src, dst_ref=dst, send_sem=ssem.at[i], recv_sem=rsem.at[i], device_id=device, device_id_type=MESH
        )

    def send(src, dst, device):
        i = used[0]
        used[0] += 1
        cp = describe(i, src, dst, device)
        cp.start()
        sent.append(cp)
        return cp, i

    loads = [
        pltpu.make_async_copy(tok_hbm, tc.at[0, pl.ds(0, 32)], lsem.at[0]),
        pltpu.make_async_copy(cot_hbm, tc.at[1, pl.ds(0, 32)], lsem.at[1]),
        pltpu.make_async_copy(win_hbm, wi, lsem.at[2]),
        pltpu.make_async_copy(wout_hbm, wo, lsem.at[3]),
        pltpu.make_async_copy(bias_hbm, bias.at[0], lsem.at[4]),
    ]
    for cp in loads:
        cp.start()

    barrier = pltpu.get_barrier_semaphore()
    greeted = [dev(dk=1)]
    for o in (1, 2, 3):
        greeted += [dev(d1=o), dev(d2=o), dev(dz=o)]
    for device in greeted:
        pl.semaphore_signal(barrier, inc=1, device_id=device, device_id_type=MESH)
    pl.semaphore_wait(barrier, len(greeted))

    def block(row):
        return tc.at[:, pl.ds(row, 32)]

    p1, p2, sib = {}, {}, {}

    def share(b):
        sib[b] = send(block(ROW[b]), block(ROW[b] + HALF[b]), dev(dk=1))[0]

    def piece(row, turn):
        return tc.at[:, pl.ds(row + 16 * turn, 16)]

    def to_first(o):
        row = ROW[(-o) % 4, 0]
        p1[(-o) % 4] = [
            send(own.at[pl.ds(16 * t, 16)], tc.at[i, pl.ds(row + 16 * t, 16)], dev(d1=o, turn=t))[0]
            for i, own in enumerate((tok_hbm, cot_hbm))
            for t in (0, 1)
        ]

    def to_far():
        p1[2] = []
        for i, (d1, o) in enumerate(((1, 3), (3, 1))):
            for t in (0, 1):
                src, dst = (tc.at[i, pl.ds(ROW[d, 0] + 16 * t, 16)] for d in (d1, 2))
                p1[2].append(send(src, dst, dev(d1=o, turn=t))[0])

    def first(d1):
        for cp in p1[d1]:
            cp.wait_recv()
        share((d1, 0))

    def to_second(src, dst, o):
        return [send(piece(ROW[src], t), piece(ROW[dst], t), dev(d2=o, turn=t))[0] for t in (0, 1)]

    def spread(d1):
        for o in (1, 3):
            d2 = (-o) % 4
            p2[d1, d2] = to_second((d1, 0), (d1, d2), o)

    def receive(d1, d2):
        for cp in p2[d1, d2]:
            cp.wait_recv()
        share((d1, d2))

    def arrive(d1, d2):
        receive(d1, d2)
        if (d2 == 1 and d1 in (0, 3)) or (d2 == 3 and d1 in (1, 2)):
            p2[d1, 2] = to_second((d1, d2), (d1, 2), (d2 + 2) % 4)

    zs, agd, fwd2 = {}, {}, {}

    def quarter(c, zz):
        n = SIZE[c] // 4
        return pl.ds(pl.multiple_of(BASE[c] + (zz % 4) * n, n), n)

    def slot(c):
        return pl.ds(BASE[c] // 4, SIZE[c] // 4)

    def forward(c):
        for b in CHUNKS[c]:
            sib[b].wait_recv()
        rows = pl.ds(BASE[c], SIZE[c])
        for i, w in enumerate((wi, wo)):
            pb[i, rows, :] = dot(tc[i, rows, :], w[...], 1, i).astype(jnp.bfloat16)
            near, far = (3, 1) if i == 0 else (1, 3)
            zs[c, i, "far"] = send(pb.at[i, quarter(c, z + 2)], za.at[i, slot(c)], dev(dz=far))[0]
            zs[c, 1 - i, "near"] = send(pb.at[i, quarter(c, z + near)], zr.at[1 - i, i, slot(c)], dev(dz=near))[0]

    def bias_out(c):
        cot = tc[1, pl.ds(BASE[c], SIZE[c]), :]
        total = jnp.sum(cot.astype(jnp.float32), axis=0, keepdims=True)
        gbout_ref[...] = total if c == 0 else gbout_ref[...] + total

    def pass_on(c):
        for i, o in enumerate((1, 3)):
            zs[c, i, "far"].wait_recv()
            there = quarter(c, z + o)
            both = pb[i, there, :].astype(jnp.float32) + za[i, slot(c), :].astype(jnp.float32)
            pb[i, there, :] = both.astype(jnp.bfloat16)
            zs[c, i, "sum"] = send(pb.at[i, there], zr.at[i, i, slot(c)], dev(dz=o))[0]

    def activate(c):
        for i in range(2):
            zs[c, i, "near"].wait_recv()
            zs[c, i, "sum"].wait_recv()
        mine = quarter(c, z)
        u = bias[...] + pb[0, mine, :].astype(jnp.float32)
        h = pb[1, mine, :].astype(jnp.float32)
        for i in range(2):
            u += zr[i, 0, slot(c), :].astype(jnp.float32)
            h += zr[i, 1, slot(c), :].astype(jnp.float32)
        activated, preact_grad = act_parts(u, h)
        ag[0, mine, :] = activated
        ag[1, mine, :] = preact_grad
        for o in (1, 3):
            agd[c, (-o) % 4] = send(ag.at[:, mine], ag.at[:, mine], dev(dz=o))[1]

    def relay(c):
        for i, s in enumerate((1, 3)):
            there = quarter(c, z + s)
            describe(agd[c, s], ag.at[:, there], ag.at[:, there], dev(dz=s)).wait_recv()
            fwd2[c, i] = send(ag.at[i, there], ag.at[i, there], dev(dz=(s + 2) % 4))[1]

    def gathered(c):
        for i in range(2):
            there = ag.at[i, quarter(c, z + 2)]
            describe(fwd2[c, i], there, there, dev(dz=2)).wait_recv()

    exd, rrd = {}, {}

    def token_grad(c):
        gathered(c)
        rows = pl.ds(BASE[c], SIZE[c])
        pg = ag[1, rows, :]

        @pl.loop(0, 2)
        def _(n):
            cols = pl.ds(pl.multiple_of(n * 1536, 1536), 1536)
            gt[rows, cols] = dot(pg, wi[cols, :], 1, 1).astype(jnp.bfloat16)

        h = SIZE[c] // 2
        exd[c] = send(gt.at[pl.ds(BASE[c] + h, h)], ex.at[pl.ds(BASE[c] // 2, h)], dev(dk=1))[0]
        total = jnp.sum(pg.astype(jnp.float32), axis=0, keepdims=True)
        gbin_ref[...] = total if c == 2 else gbin_ref[...] + total

    def combine(c):
        exd[c].wait_recv()
        h = SIZE[c] // 2
        own = pl.ds(BASE[c], h)
        other = ex[pl.ds(BASE[c] // 2, h), :].astype(jnp.float32)
        gt[own, :] = (gt[own, :].astype(jnp.float32) + other).astype(jnp.bfloat16)
        for d1, d2 in CHUNKS[c]:
            if d2:
                rrd[d1, d2] = []
                for t in (0, 1):
                    src = gt.at[pl.ds(ROW[d1, d2] + 16 * t, 16)]
                    dst = rr.at[(-d2) % 4 - 1, pl.ds(D1.index(d1) * 32 + 16 * t, 16)]
                    rrd[d1, d2].append(send(src, dst, dev(d2=d2, turn=t))[0])

    def end_scatter(d1):
        total = gt[pl.ds(ROW[d1, 0], 32), :].astype(jnp.float32)
        for d2 in (1, 3, 2):
            for cp in rrd[d1, d2]:
                cp.wait_recv()
            total += rr[(-d2) % 4 - 1, pl.ds(D1.index(d1) * 32, 32), :].astype(jnp.float32)
        if d1 == 0:
            fin[...] = total
        else:
            q2[d1 - 1] = total.astype(jnp.bfloat16)
            for t in (0, 1):
                rows = pl.ds(16 * t, 16)
                r2d.append(send(q2.at[d1 - 1, rows], r2.at[(-d1) % 4 - 1, rows], dev(d1=d1, turn=t))[0])

    def weight_out_part(n):
        cols, late = pl.ds(n * 768, 768), pl.ds(512, 512)
        acc[:, cols] = dot(ag[0, late, :], tc[1, late, cols], 0, 0)

    def weight_out_grad(n):
        cols, early = pl.ds(n * 768, 768), pl.ds(0, 512)
        total = acc[:, cols] + dot(ag[0, early, :], tc[1, early, cols], 0, 0)
        wo[:, cols] = total.astype(jnp.bfloat16)

    def weight_in_grad(n):
        cols = pl.ds(n * 768, 768)
        wi[cols, :] = dot(tc[0, :, cols], ag[1], 0, 0).astype(jnp.bfloat16)

    r2d = []
    to_first(1)
    to_first(3)
    loads[0].wait()
    loads[1].wait()
    share((0, 0))
    first(1)
    first(3)
    to_far()
    spread(0)
    spread(1)
    spread(3)
    loads[2].wait()
    loads[3].wait()
    loads[4].wait()
    forward(0)
    first(2)
    spread(2)
    arrive(0, 1)
    arrive(0, 3)
    pass_on(0)
    forward(1)
    activate(0)
    bias_out(0)
    arrive(1, 1)
    arrive(1, 3)
    pass_on(1)
    arrive(3, 1)
    arrive(3, 3)
    forward(2)
    activate(1)
    bias_out(1)
    receive(0, 2)
    receive(1, 2)
    pass_on(2)
    arrive(2, 1)
    arrive(2, 3)
    forward(3)
    activate(2)
    bias_out(2)
    receive(3, 2)
    receive(2, 2)
    pass_on(3)
    relay(2)
    forward(4)
    activate(3)
    pass_on(4)
    bias_out(3)
    token_grad(2)
    relay(3)
    activate(4)
    combine(2)
    relay(1)
    token_grad(3)
    relay(4)
    weight_out_part(0)
    combine(3)
    relay(0)
    weight_out_part(1)
    token_grad(4)
    weight_out_part(2)
    combine(4)
    token_grad(1)
    weight_out_part(3)
    token_grad(0)
    combine(1)
    bias_out(4)
    combine(0)
    end_scatter(1)
    end_scatter(0)
    weight_out_grad(0)
    end_scatter(2)
    end_scatter(3)
    weight_out_grad(1)
    weight_out_grad(2)
    weight_out_grad(3)
    for n in range(4):
        weight_in_grad(n)
    for cp in r2d:
        cp.wait_recv()
    total = fin[...]
    for s in range(3):
        total += r2[s].astype(jnp.float32)
    gtok_ref[...] = total.astype(jnp.bfloat16)
    for cp in sent:
        cp.wait_send()


def store(*refs):
    sem = refs[10]
    moves = [pltpu.make_async_copy(refs[i], refs[5 + i], sem.at[i]) for i in (1, 3, 0)]
    moves += [pltpu.make_async_copy(refs[i].at[0], refs[5 + i], sem.at[i]) for i in (2, 4)]
    for cp in moves:
        cp.start()
    for cp in moves:
        cp.wait()


def per_device(tokens, cotangent, weight_in, bias_in, weight_out):
    hbm = pl.BlockSpec(memory_space=pl.ANY)
    bf16, f32 = jnp.bfloat16, jnp.float32
    kept = (((32, 3072), bf16), ((3072, 768), bf16), ((1, 768), f32), ((768, 3072), bf16), ((1, 3072), f32))
    results = pl.pallas_call(
        kernel,
        out_shape=tuple(pltpu.VMEM(shape, dtype) for shape, dtype in kept),
        in_specs=[hbm] * 5,
        out_specs=tuple(pl.BlockSpec(memory_space=pltpu.VMEM) for _ in kept),
        scratch_shapes=[
            pltpu.VMEM((1, 768), f32),
            pltpu.VMEM((2, 1024, 3072), bf16),
            pltpu.VMEM((2, 1024, 768), bf16),
            pltpu.VMEM((2, 256, 768), bf16),
            pltpu.VMEM((2, 2, 256, 768), bf16),
            pltpu.VMEM((2, 1024, 768), bf16),
            pltpu.VMEM((1024, 3072), bf16),
            pltpu.VMEM((512, 3072), bf16),
            pltpu.VMEM((3, 128, 3072), bf16),
            pltpu.VMEM((3, 32, 3072), bf16),
            pltpu.VMEM((3, 32, 3072), bf16),
            pltpu.VMEM((32, 3072), f32),
            pltpu.VMEM((768, 3072), f32),
            pltpu.SemaphoreType.DMA((5,)),
            pltpu.SemaphoreType.DMA((N_COPIES,)),
            pltpu.SemaphoreType.DMA((N_COPIES,)),
        ],
        compiler_params=pltpu.CompilerParams(
            collective_id=0, has_side_effects=True, vmem_limit_bytes=50 * 2**20
        ),
        cost_estimate=pl.CostEstimate(flops=24_200_000_000, bytes_accessed=20_000_000, transcendentals=800_000),
    )(tokens, cotangent, weight_in, bias_in, weight_out)
    return pl.pallas_call(
        store,
        out_shape=tuple(
            jax.ShapeDtypeStruct(shape[1:] if shape[0] == 1 else shape, dtype) for shape, dtype in kept
        ),
        in_specs=[pl.BlockSpec(memory_space=pltpu.VMEM)] * 5,
        out_specs=(hbm,) * 5,
        scratch_shapes=[pltpu.SemaphoreType.DMA((5,))],
        compiler_params=pltpu.CompilerParams(vmem_limit_bytes=2**20),
    )(*results)


def solution(mesh):
    placed = (P("col", "row"), P("col", "row"), P("row", "col"), P("col"), P("col", "row"))
    return jax.shard_map(
        per_device,
        mesh=mesh,
        in_specs=placed,
        out_specs=(P("col", "row"), P("row", "col"), P("col"), P("col", "row"), P("row")),
        check_vma=False,
    )
```

```python
import jax
import jax.numpy as jnp
from jax import lax
from jax.experimental import pallas as pl
from jax.experimental.pallas import tpu as pltpu
from jax.sharding import PartitionSpec as P

MESH = pl.DeviceIdType.MESH
coeff = 0.7978845608
N_COPIES = 160
D1 = (0, 1, 3, 2)
CHUNKS = (
    ((0, 0), (1, 0), (3, 0)),
    ((2, 0), (0, 1), (0, 3)),
    ((1, 1), (1, 3), (2, 1), (2, 3)),
    ((0, 2), (1, 2), (3, 1), (3, 3)),
    ((3, 2), (2, 2)),
)
SIZE = [64 * len(blocks) for blocks in CHUNKS]
ORDER = (0, 1, 4, 2, 3)
BASE = {c: sum(SIZE[d] for d in ORDER[:i]) for i, c in enumerate(ORDER)}
ROW = {b: BASE[c] + i * 32 for c, blocks in enumerate(CHUNKS) for i, b in enumerate(blocks)}
HALF = {b: SIZE[c] // 2 for c, blocks in enumerate(CHUNKS) for b in blocks}


def act_parts(preact, hidden_grad):
    cube = preact * preact * preact
    tangent = jnp.tanh(coeff * (preact + 0.044715 * cube))
    activated = (0.5 * preact * (1.0 + tangent)).astype(jnp.bfloat16)
    slope = 0.5 * (1.0 + tangent) + 0.5 * preact * (1.0 - tangent * tangent) * coeff * (
        1.0 + 0.134145 * preact * preact
    )
    return (activated, (hidden_grad * slope).astype(jnp.bfloat16))


def dot(a, b, ca, cb):
    return lax.dot_general(a, b, (((ca,), (cb,)), ((), ())), preferred_element_type=jnp.float32)


def kernel(
    tok_hbm, cot_hbm, win_hbm, bias_hbm, wout_hbm,
    gtok_ref, wi, gbin_ref, wo, gbout_ref,
    bias, tc, pb, za, zr, ag, gt, ex, rr, q2, r2, fin, acc, lsem, ssem, rsem,
):
    z = lax.axis_index("row")
    col = lax.axis_index("col")
    y, x, k = col // 8, (col // 2) % 4, col % 2

    def dev(d1=0, d2=0, dz=0, dk=0, turn=0):
        dx, dy = (d2, d1) if turn else (d1, d2)
        return ((z + dz) % 4, ((y + dy) % 4) * 8 + ((x + dx) % 4) * 2 + (k + dk) % 2)

    used = [0]
    sent = []

    def describe(i, src, dst, device):
        return pltpu.make_async_remote_copy(
            src_ref=src, dst_ref=dst, send_sem=ssem.at[i], recv_sem=rsem.at[i], device_id=device, device_id_type=MESH
        )

    def send(src, dst, device):
        i = used[0]
        used[0] += 1
        cp = describe(i, src, dst, device)
        cp.start()
        sent.append(cp)
        return cp, i

    loads = [
        pltpu.make_async_copy(tok_hbm, tc.at[0, pl.ds(0, 32)], lsem.at[0]),
        pltpu.make_async_copy(cot_hbm, tc.at[1, pl.ds(0, 32)], lsem.at[1]),
        pltpu.make_async_copy(win_hbm, wi, lsem.at[2]),
        pltpu.make_async_copy(wout_hbm, wo, lsem.at[3]),
        pltpu.make_async_copy(bias_hbm, bias.at[0], lsem.at[4]),
    ]
    for cp in loads:
        cp.start()

    barrier = pltpu.get_barrier_semaphore()
    greeted = [dev(dk=1)]
    for o in (1, 2, 3):
        greeted += [dev(d1=o), dev(d2=o), dev(dz=o)]
    for device in greeted:
        pl.semaphore_signal(barrier, inc=1, device_id=device, device_id_type=MESH)
    pl.semaphore_wait(barrier, len(greeted))

    def block(row):
        return tc.at[:, pl.ds(row, 32)]

    p1, p2, sib = {}, {}, {}

    def share(b):
        sib[b] = send(block(ROW[b]), block(ROW[b] + HALF[b]), dev(dk=1))[0]

    def piece(row, turn):
        return tc.at[:, pl.ds(row + 16 * turn, 16)]

    def to_first(o):
        row = ROW[(-o) % 4, 0]
        p1[(-o) % 4] = [
            send(own.at[pl.ds(16 * t, 16)], tc.at[i, pl.ds(row + 16 * t, 16)], dev(d1=o, turn=t))[0]
            for i, own in enumerate((tok_hbm, cot_hbm))
            for t in (0, 1)
        ]

    def to_far():
        p1[2] = []
        for i, (d1, o) in enumerate(((1, 3), (3, 1))):
            for t in (0, 1):
                src, dst = (tc.at[i, pl.ds(ROW[d, 0] + 16 * t, 16)] for d in (d1, 2))
                p1[2].append(send(src, dst, dev(d1=o, turn=t))[0])

    def first(d1):
        for cp in p1[d1]:
            cp.wait_recv()
        share((d1, 0))

    def to_second(src, dst, o):
        return [send(piece(ROW[src], t), piece(ROW[dst], t), dev(d2=o, turn=t))[0] for t in (0, 1)]

    def spread(d1):
        for o in (1, 3):
            d2 = (-o) % 4
            p2[d1, d2] = to_second((d1, 0), (d1, d2), o)

    def receive(d1, d2):
        for cp in p2[d1, d2]:
            cp.wait_recv()
        share((d1, d2))

    def arrive(d1, d2):
        receive(d1, d2)
        if (d2 == 1 and d1 in (0, 3)) or (d2 == 3 and d1 in (1, 2)):
            p2[d1, 2] = to_second((d1, d2), (d1, 2), (d2 + 2) % 4)

    zs, agd, fwd2 = {}, {}, {}

    def quarter(c, zz):
        n = SIZE[c] // 4
        return pl.ds(pl.multiple_of(BASE[c] + (zz % 4) * n, n), n)

    def slot(c):
        return pl.ds(BASE[c] // 4, SIZE[c] // 4)

    def forward(c):
        for b in CHUNKS[c]:
            sib[b].wait_recv()
        rows = pl.ds(BASE[c], SIZE[c])
        for i, w in enumerate((wi, wo)):
            pb[i, rows, :] = dot(tc[i, rows, :], w[...], 1, i).astype(jnp.bfloat16)
            near, far = (3, 1) if i == 0 else (1, 3)
            zs[c, i, "far"] = send(pb.at[i, quarter(c, z + 2)], za.at[i, slot(c)], dev(dz=far))[0]
            zs[c, 1 - i, "near"] = send(pb.at[i, quarter(c, z + near)], zr.at[1 - i, i, slot(c)], dev(dz=near))[0]

    def bias_out(c):
        cot = tc[1, pl.ds(BASE[c], SIZE[c]), :]
        total = jnp.sum(cot.astype(jnp.float32), axis=0, keepdims=True)
        gbout_ref[...] = total if c == 0 else gbout_ref[...] + total

    def pass_on(c):
        for i, o in enumerate((1, 3)):
            zs[c, i, "far"].wait_recv()
            there = quarter(c, z + o)
            both = pb[i, there, :].astype(jnp.float32) + za[i, slot(c), :].astype(jnp.float32)
            pb[i, there, :] = both.astype(jnp.bfloat16)
            zs[c, i, "sum"] = send(pb.at[i, there], zr.at[i, i, slot(c)], dev(dz=o))[0]

    def activate(c):
        for i in range(2):
            zs[c, i, "near"].wait_recv()
            zs[c, i, "sum"].wait_recv()
        mine = quarter(c, z)
        u = bias[...] + pb[0, mine, :].astype(jnp.float32)
        h = pb[1, mine, :].astype(jnp.float32)
        for i in range(2):
            u += zr[i, 0, slot(c), :].astype(jnp.float32)
            h += zr[i, 1, slot(c), :].astype(jnp.float32)
        activated, preact_grad = act_parts(u, h)
        ag[0, mine, :] = activated
        ag[1, mine, :] = preact_grad
        for o in (1, 3):
            agd[c, (-o) % 4] = send(ag.at[:, mine], ag.at[:, mine], dev(dz=o))[1]

    def relay(c):
        for i, s in enumerate((1, 3)):
            there = quarter(c, z + s)
            describe(agd[c, s], ag.at[:, there], ag.at[:, there], dev(dz=s)).wait_recv()
            fwd2[c, i] = send(ag.at[i, there], ag.at[i, there], dev(dz=(s + 2) % 4))[1]

    def gathered(c):
        for i in range(2):
            there = ag.at[i, quarter(c, z + 2)]
            describe(fwd2[c, i], there, there, dev(dz=2)).wait_recv()

    exd, rrd = {}, {}

    def token_grad(c):
        gathered(c)
        rows = pl.ds(BASE[c], SIZE[c])
        pg = ag[1, rows, :]

        @pl.loop(0, 2)
        def _(n):
            cols = pl.ds(pl.multiple_of(n * 1536, 1536), 1536)
            gt[rows, cols] = dot(pg, wi[cols, :], 1, 1).astype(jnp.bfloat16)

        h = SIZE[c] // 2
        exd[c] = send(gt.at[pl.ds(BASE[c] + h, h)], ex.at[pl.ds(BASE[c] // 2, h)], dev(dk=1))[0]
        total = jnp.sum(pg.astype(jnp.float32), axis=0, keepdims=True)
        gbin_ref[...] = total if c == 2 else gbin_ref[...] + total

    def combine(c):
        exd[c].wait_recv()
        h = SIZE[c] // 2
        own = pl.ds(BASE[c], h)
        other = ex[pl.ds(BASE[c] // 2, h), :].astype(jnp.float32)
        gt[own, :] = (gt[own, :].astype(jnp.float32) + other).astype(jnp.bfloat16)
        for d1, d2 in CHUNKS[c]:
            if d2:
                rrd[d1, d2] = []
                for t in (0, 1):
                    src = gt.at[pl.ds(ROW[d1, d2] + 16 * t, 16)]
                    dst = rr.at[(-d2) % 4 - 1, pl.ds(D1.index(d1) * 32 + 16 * t, 16)]
                    rrd[d1, d2].append(send(src, dst, dev(d2=d2, turn=t))[0])

    def end_scatter(d1):
        total = gt[pl.ds(ROW[d1, 0], 32), :].astype(jnp.float32)
        for d2 in (1, 3, 2):
            for cp in rrd[d1, d2]:
                cp.wait_recv()
            total += rr[(-d2) % 4 - 1, pl.ds(D1.index(d1) * 32, 32), :].astype(jnp.float32)
        if d1 == 0:
            fin[...] = total
        else:
            q2[d1 - 1] = total.astype(jnp.bfloat16)
            for t in (0, 1):
                rows = pl.ds(16 * t, 16)
                r2d.append(send(q2.at[d1 - 1, rows], r2.at[(-d1) % 4 - 1, rows], dev(d1=d1, turn=t))[0])

    def weight_out_part(n):
        cols, late = pl.ds(n * 768, 768), pl.ds(512, 512)
        acc[:, cols] = dot(ag[0, late, :], tc[1, late, cols], 0, 0)

    def weight_out_grad(n):
        cols, early = pl.ds(n * 768, 768), pl.ds(0, 512)
        total = acc[:, cols] + dot(ag[0, early, :], tc[1, early, cols], 0, 0)
        wo[:, cols] = total.astype(jnp.bfloat16)

    def weight_in_grad(n):
        cols = pl.ds(n * 768, 768)
        wi[cols, :] = dot(tc[0, :, cols], ag[1], 0, 0).astype(jnp.bfloat16)

    r2d = []
    to_first(1)
    to_first(3)
    loads[0].wait()
    loads[1].wait()
    share((0, 0))
    first(1)
    first(3)
    to_far()
    spread(0)
    loads[2].wait()
    loads[3].wait()
    loads[4].wait()
    forward(0)
    spread(1)
    first(2)
    spread(2)
    spread(3)
    arrive(0, 1)
    arrive(0, 3)
    pass_on(0)
    forward(1)
    arrive(1, 1)
    arrive(1, 3)
    activate(0)
    pass_on(1)
    arrive(2, 1)
    arrive(2, 3)
    forward(2)
    arrive(3, 1)
    arrive(3, 3)
    activate(1)
    pass_on(2)
    receive(0, 2)
    receive(1, 2)
    forward(3)
    activate(2)
    receive(3, 2)
    receive(2, 2)
    pass_on(3)
    relay(2)
    forward(4)
    activate(3)
    pass_on(4)
    bias_out(0)
    token_grad(2)
    relay(3)
    activate(4)
    combine(2)
    relay(1)
    bias_out(1)
    token_grad(3)
    relay(4)
    weight_out_part(0)
    combine(3)
    relay(0)
    weight_out_part(1)
    bias_out(2)
    token_grad(4)
    weight_out_part(2)
    combine(4)
    bias_out(3)
    token_grad(1)
    weight_out_part(3)
    bias_out(4)
    token_grad(0)
    combine(1)
    combine(0)
    end_scatter(1)
    end_scatter(0)
    weight_out_grad(0)
    end_scatter(2)
    end_scatter(3)
    weight_out_grad(1)
    weight_out_grad(2)
    weight_out_grad(3)
    for n in range(4):
        weight_in_grad(n)
    for cp in r2d:
        cp.wait_recv()
    total = fin[...]
    for s in range(3):
        total += r2[s].astype(jnp.float32)
    gtok_ref[...] = total.astype(jnp.bfloat16)
    for cp in sent:
        cp.wait_send()


def store(*refs):
    sem = refs[10]
    moves = [pltpu.make_async_copy(refs[i], refs[5 + i], sem.at[i]) for i in (1, 3, 0)]
    moves += [pltpu.make_async_copy(refs[i].at[0], refs[5 + i], sem.at[i]) for i in (2, 4)]
    for cp in moves:
        cp.start()
    for cp in moves:
        cp.wait()


def per_device(tokens, cotangent, weight_in, bias_in, weight_out):
    hbm = pl.BlockSpec(memory_space=pl.ANY)
    bf16, f32 = jnp.bfloat16, jnp.float32
    kept = (((32, 3072), bf16), ((3072, 768), bf16), ((1, 768), f32), ((768, 3072), bf16), ((1, 3072), f32))
    results = pl.pallas_call(
        kernel,
        out_shape=tuple(pltpu.VMEM(shape, dtype) for shape, dtype in kept),
        in_specs=[hbm] * 5,
        out_specs=tuple(pl.BlockSpec(memory_space=pltpu.VMEM) for _ in kept),
        scratch_shapes=[
            pltpu.VMEM((1, 768), f32),
            pltpu.VMEM((2, 1024, 3072), bf16),
            pltpu.VMEM((2, 1024, 768), bf16),
            pltpu.VMEM((2, 256, 768), bf16),
            pltpu.VMEM((2, 2, 256, 768), bf16),
            pltpu.VMEM((2, 1024, 768), bf16),
            pltpu.VMEM((1024, 3072), bf16),
            pltpu.VMEM((512, 3072), bf16),
            pltpu.VMEM((3, 128, 3072), bf16),
            pltpu.VMEM((3, 32, 3072), bf16),
            pltpu.VMEM((3, 32, 3072), bf16),
            pltpu.VMEM((32, 3072), f32),
            pltpu.VMEM((768, 3072), f32),
            pltpu.SemaphoreType.DMA((5,)),
            pltpu.SemaphoreType.DMA((N_COPIES,)),
            pltpu.SemaphoreType.DMA((N_COPIES,)),
        ],
        compiler_params=pltpu.CompilerParams(
            collective_id=0, has_side_effects=True, vmem_limit_bytes=50 * 2**20
        ),
        cost_estimate=pl.CostEstimate(flops=24_200_000_000, bytes_accessed=20_000_000, transcendentals=800_000),
    )(tokens, cotangent, weight_in, bias_in, weight_out)
    return pl.pallas_call(
        store,
        out_shape=tuple(
            jax.ShapeDtypeStruct(shape[1:] if shape[0] == 1 else shape, dtype) for shape, dtype in kept
        ),
        in_specs=[pl.BlockSpec(memory_space=pltpu.VMEM)] * 5,
        out_specs=(hbm,) * 5,
        scratch_shapes=[pltpu.SemaphoreType.DMA((5,))],
        compiler_params=pltpu.CompilerParams(vmem_limit_bytes=2**20),
    )(*results)


def solution(mesh):
    placed = (P("col", "row"), P("col", "row"), P("row", "col"), P("col"), P("col", "row"))
    return jax.shard_map(
        per_device,
        mesh=mesh,
        in_specs=placed,
        out_specs=(P("col", "row"), P("row", "col"), P("col"), P("col", "row"), P("row")),
        check_vma=False,
    )
```
